32 devices in a mesh: row: 8 (over z, y), col: 2 (over x), depth: 2 (over core).
Axes of the slice: x: 2, y: 2, z: 4, core: 2. Of those that a mesh axis runs over, the one named last changes fastest.
Arguments:
- upper_tiles: bfloat16 [1024, 5, 128, 128], P(('row', 'col')), may hold values from -6 to 6
- upper_cols: int32 [1024, 5], P(('row', 'col')), may hold values from -1 to 1023, as said below
Outputs:
- new_tiles: bfloat16 [1024, 5, 128, 128], P(('row', 'col'), None, 'depth')
The draws below stay inside these ranges and needn't reach their ends.
Inputs may be any that keep to these rules, and one draw needn't show every extreme that they name: upper_cols[i, o] is (i + o) mod 1024 where block row i holds a block at offset o and -1 where it holds none; offset 0 is always held.
All inputs are finite; a program needn't handle non-finite values.
Results may differ from the reference program's by a relative error of at most 0.0036.
Values may be sent and summed in bfloat16 or wider, within the bound.
A program may use at most 256 MiB of HBM per device.

```python
import jax
import jax.numpy as jnp

BS = 128
NB = 1024
H = 4
U = 5


def draw_upper_cols(key, part):
    row_index = jnp.arange(NB, dtype=jnp.int32)[:, None]
    offsets = jnp.arange(H + 1, dtype=jnp.int32)[None, :]
    columns = (row_index + offsets) % NB
    chance = jax.random.randint(key, (NB, H + 1), 0, 20)
    keep = (chance < 17) | (offsets == 0)
    return jnp.where(keep, columns, -1).astype(jnp.int32)


def block_levels(own_key, shape, shards, low, high):
    def one(position, shards_of):
        draws = jax.random.uniform(jax.random.fold_in(jax.random.fold_in(own_key, 6), position), (shards_of,), jnp.float32, low / len(shards), high / len(shards))
        return jnp.repeat(jnp.exp(draws), shape[position] // shards_of).reshape((-1,) + (1,) * (len(shape) - position - 1))

    factor_of = one(*shards[0])
    for cut in shards[1:]:
        factor_of = factor_of * one(*cut)
    return factor_of


def noise(rng, extent, spread, most, split=(), held_as=jnp.bfloat16):
    level = block_levels(rng, extent, split, -0.22, 0.18) if split else 1.0
    array = jax.random.normal(rng, extent, jnp.float32) * spread * level
    return jnp.minimum(jnp.maximum(array, -most), most).astype(held_as)


def setup_inputs(seed: int = 0) -> dict:
    key_list = jax.random.split(jax.random.key(seed), 3)
    upper_tiles = noise(key_list[0], (NB, U, BS, BS), 1.0, 6.0, ((0, 16),))
    upper_cols = draw_upper_cols(jax.random.fold_in(key_list[2], 71), 0)
    return {"upper_tiles": upper_tiles, "upper_cols": upper_cols}


def mirror_diagonal(blocks):
    upper_part = jnp.triu(blocks)
    strict_part = jnp.triu(blocks, 1)
    return upper_part + jnp.swapaxes(strict_part, -1, -2)


def expand_rows(stored):
    lower_part = [jnp.swapaxes(jnp.roll(stored[:, shift_by], shift_by, axis=0), -1, -2) for shift_by in range(H, 0, -1)]
    return jnp.concatenate([jnp.stack(lower_part, axis=1), stored], axis=1)


def band_sum(left_full, right_full, target):
    total = jnp.zeros((NB, BS, BS), jnp.float32)
    for middle in range(target - H, H + 1):
        factor = left_full[:, H + middle].astype(jnp.float32)
        partner = jnp.roll(right_full[:, H + target - middle], -middle, axis=0).astype(jnp.float32)
        total = total + jnp.einsum("rab,rbc->rac", factor, partner)
    return total


def reference(upper_tiles, upper_cols):
    scale_sq = 1.0 / (2.0 * (2 * H + 1) * BS)
    present = upper_cols >= 0
    masked = jnp.where(present[:, :, None, None], upper_tiles, jnp.zeros_like(upper_tiles))
    stored = jnp.concatenate([mirror_diagonal(masked[:, :1]), masked[:, 1:]], axis=1)
    full_rows = expand_rows(stored)
    square_list = []
    for target in range(H + 1):
        square_list.append((band_sum(full_rows, full_rows, target) * scale_sq).astype(jnp.bfloat16))
    square = jnp.stack(square_list, axis=1)
    square_full = expand_rows(square)
    result_list = []
    for target in range(H + 1):
        linear_term = full_rows[:, H + target].astype(jnp.float32)
        value = 1.5 * linear_term - 0.5 * band_sum(full_rows, square_full, target)
        value = jnp.where(present[:, target][:, None, None], value, jnp.float32(0.0))
        result_list.append(value.astype(jnp.bfloat16))
    return jnp.stack(result_list, axis=1)
```

```python
import functools

import jax
import jax.numpy as jnp
from jax import lax
from jax.experimental import pallas as pl
from jax.experimental.pallas import tpu as pltpu
from jax.sharding import PartitionSpec as P

MESH = pl.DeviceIdType.MESH
NT = (((1,), (1,)), ((), ()))
NN = (((1,), (0,)), ((), ()))


def matmul(left, right, dims):
    return lax.dot_general(left, right, dims, preferred_element_type=jnp.float32)


def kernel(
    groups,
    cols_size,
    own_pairs,
    block,
    scale_sq,
    tiles_ref,
    mask_ref,
    out_ref,
    held,
    mask,
    band,
    square,
    staged,
    local_sem,
    mask_sem,
    halo_send,
    halo_recv,
    mask_send,
    mask_recv,
    keep_sem,
    give_send,
    give_recv,
):
    pairs = own_pairs + 4
    wide = 2 * block
    half_rows = 2 * own_pairs
    depth = lax.axis_index("depth")
    place = lax.axis_index("row") * cols_size + lax.axis_index("col")
    after = lax.rem(place + 1, groups)
    before = lax.rem(place + groups - 1, groups)

    def device(group, layer):
        return (group // cols_size, lax.rem(group, cols_size), layer)

    barrier = pltpu.get_barrier_semaphore()
    for other in (device(after, depth), device(before, depth), device(place, 1 - depth)):
        pl.semaphore_signal(barrier, inc=1, device_id=other, device_id_type=MESH)

    local_count = half_rows + 4
    local_from = depth * (half_rows - 4)
    local_to = 4 * (1 - depth)
    own_copy = pltpu.make_async_copy(
        tiles_ref.at[pl.ds(local_from, local_count)],
        held.at[pl.ds(local_to, local_count)],
        local_sem,
    )
    own_copy.start()
    own_mask = pltpu.make_async_copy(
        mask_ref.at[pl.ds(local_from, local_count)],
        mask.at[pl.ds(local_to, local_count)],
        mask_sem,
    )
    own_mask.start()
    pl.semaphore_wait(barrier, 3)

    partner = jnp.where(depth == 0, after, before)
    give_from = (1 - depth) * (2 * half_rows - 4)
    give_to = depth * (half_rows + 4)
    halo = pltpu.make_async_remote_copy(
        src_ref=tiles_ref.at[pl.ds(give_from, 4)],
        dst_ref=held.at[pl.ds(give_to, 4)],
        send_sem=halo_send,
        recv_sem=halo_recv,
        device_id=device(partner, depth),
        device_id_type=MESH,
    )
    halo.start()
    halo_mask = pltpu.make_async_remote_copy(
        src_ref=mask_ref.at[pl.ds(give_from, 4)],
        dst_ref=mask.at[pl.ds(give_to, 4)],
        send_sem=mask_send,
        recv_sem=mask_recv,
        device_id=device(partner, depth),
        device_id_type=MESH,
    )
    halo_mask.start()
    own_mask.wait()
    own_copy.wait()

    def spread(pair, carry):
        zero = jnp.zeros((block, block), jnp.bfloat16)
        band[pair, 0:block, 9 * block : 10 * block] = zero
        band[pair, block:wide, 0:block] = zero
        for a in range(2):
            for o in range(5):
                values = held[2 * pair + a, o].astype(jnp.float32)
                present = mask[2 * pair + a, o : o + 1, :]
                values = jnp.where(present > 0, values, 0.0)
                if o == 0:
                    down = lax.broadcasted_iota(jnp.int32, (block, block), 0)
                    along = lax.broadcasted_iota(jnp.int32, (block, block), 1)
                    values = jnp.where(down <= along, values, values.T)
                values = values.astype(jnp.bfloat16)
                at = (a + o + 4) * block
                band[pair, a * block : (a + 1) * block, at : at + block] = values
                if o > 0:
                    step, b = divmod(a + o, 2)
                    at = (a - 2 * step + 4) * block
                    band[pair + step, b * block : (b + 1) * block, at : at + block] = values.T
        return carry

    def square_tile(pair, e):
        total = matmul(band[pair, :, e * wide :], band[pair + e, :, : (5 - e) * wide], NT)
        tile = (total * scale_sq).astype(jnp.bfloat16)
        square[pair, :, e * wide : (e + 1) * wide] = tile
        if e == 2:
            square[pair, 0:block, 5 * block : 6 * block] = jnp.zeros((block, block), jnp.bfloat16)

    def square_row(pair, carry):
        for e in range(3):
            square_tile(pair, e)
        return carry

    def keep(own):
        rows = pl.ds(2 * own, 2)
        return pltpu.make_async_copy(
            staged.at[rows, :, depth],
            out_ref.at[pl.ds(depth * half_rows + 2 * own, 2)],
            keep_sem.at[own],
        )

    def give(own):
        rows = pl.ds(2 * own, 2)
        return pltpu.make_async_remote_copy(
            src_ref=staged.at[rows, :, 1 - depth],
            dst_ref=out_ref.at[pl.ds(depth * half_rows + 2 * own, 2)],
            send_sem=give_send.at[own],
            recv_sem=give_recv.at[own],
            device_id=device(place, 1 - depth),
            device_id_type=MESH,
        )

    def out_row(own, carry):
        pair = own + 2
        for e in range(3):
            k = pair + e
            total = matmul(band[pair, :, (e + 2) * wide :], square[k, :, : (3 - e) * wide], NT)
            total += matmul(
                band[pair, :, e * wide : (e + 1) * wide], square[k - 2, :, 2 * wide : 3 * wide], NN
            )
            total += matmul(
                band[pair, :, (e + 1) * wide : (e + 2) * wide], square[k - 1, :, wide : 2 * wide], NN
            )
            for a in range(2):
                for b in range(2):
                    o = 2 * e + b - a
                    if 0 <= o <= 4:
                        product = total[a * block : (a + 1) * block, b * block : (b + 1) * block]
                        at = (a + o + 4) * block
                        linear = band[pair, a * block : (a + 1) * block, at : at + block]
                        value = 1.5 * linear.astype(jnp.float32) - 0.5 * product
                        present = mask[2 * pair + a, o : o + 1, :]
                        value = jnp.where(present > 0, value, 0.0).astype(jnp.bfloat16)
                        for part in range(2):
                            staged[2 * own + a, o, part] = value[
                                part * block // 2 : (part + 1) * block // 2
                            ]
        keep(own).start()
        give(own).start()
        return carry

    low = 2 * (1 - depth)
    lax.fori_loop(low, low + own_pairs + 2, spread, 0)
    lax.fori_loop(2 + low, own_pairs + low, square_row, 0)
    halo.wait()
    halo_mask.wait()
    late = depth * (own_pairs + 2)
    lax.fori_loop(late, late + 2, spread, 0)
    late_square = 2 + depth * (own_pairs - 2)
    lax.fori_loop(late_square, late_square + 2, square_row, 0)
    for pair, e in ((0, 2), (1, 1), (1, 2)):
        square_tile(pair, e)
    for pair, e in ((2, 0), (2, 1), (3, 0)):
        square_tile(own_pairs + pair, e)
    lax.fori_loop(0, own_pairs, out_row, 0)

    def finish(own, carry):
        keep(own).wait()
        give(own).wait()
        return carry

    lax.fori_loop(0, own_pairs, finish, 0)


def per_device(upper_tiles, upper_cols):
    rows, offsets, block, _ = upper_tiles.shape
    reach = offsets - 1
    scale_sq = 1.0 / (2.0 * (2 * reach + 1) * block)
    cols_size = lax.axis_size("col")
    groups = lax.axis_size("row") * cols_size
    own_pairs = rows // 4
    pairs = own_pairs + 4
    present = (upper_cols >= 0).astype(jnp.float32)
    present = jnp.pad(present, ((0, 0), (0, 8 - offsets)))
    present = jnp.broadcast_to(present[:, :, None], (rows, 8, 128))
    body = functools.partial(kernel, groups, cols_size, own_pairs, block, scale_sq)
    dma = pltpu.SemaphoreType.DMA
    return pl.pallas_call(
        body,
        out_shape=jax.ShapeDtypeStruct((rows, offsets, block // 2, block), jnp.bfloat16),
        in_specs=[pl.BlockSpec(memory_space=pl.ANY)] * 2,
        out_specs=pl.BlockSpec(memory_space=pl.ANY),
        scratch_shapes=[
            pltpu.VMEM((2 * pairs, offsets, block, block), jnp.bfloat16),
            pltpu.VMEM((2 * pairs, 8, 128), jnp.float32),
            pltpu.VMEM((pairs + 2, 2 * block, 10 * block), jnp.bfloat16),
            pltpu.VMEM((pairs, 2 * block, 6 * block), jnp.bfloat16),
            pltpu.VMEM((2 * own_pairs, offsets, 2, block // 2, block), jnp.bfloat16),
            dma,
            dma,
            dma,
            dma,
            dma,
            dma,
            dma((own_pairs,)),
            dma((own_pairs,)),
            dma((own_pairs,)),
        ],
        compiler_params=pltpu.CompilerParams(
            collective_id=0, has_side_effects=True, vmem_limit_bytes=56 * 1024 * 1024
        ),
        cost_estimate=pl.CostEstimate(
            flops=14_000_000_000, bytes_accessed=20_000_000, transcendentals=0
        ),
    )(upper_tiles, present)


def solution(mesh):
    placed = (P(("row", "col"), None, None, None), P(("row", "col"), None))
    return jax.shard_map(
        per_device,
        mesh=mesh,
        in_specs=placed,
        out_specs=P(("row", "col"), None, "depth", None),
        check_vma=False,
    )
```
